512 devices in a mesh: ctx: 64 (over y_lo, z, core), mp: 8 (over x, y_hi).
Axes of the slice: x: 4, y: 8 (y_hi: 2, y_lo: 4; y = y_hi * 4 + y_lo), z: 8, core: 2. Of those that a mesh axis runs over, the one named last changes fastest.
Arguments:
- queries: bfloat16 [16384, 5120], P('ctx', 'mp'), may hold values from -10 to 10
- keys: bfloat16 [16384, 1024], P('ctx', 'mp'), may hold values from -20 to 20
- values: bfloat16 [16384, 1024], P('ctx', 'mp'), may hold values from -6 to 6
- kept_rows: int32 [64, 8, 128], P('ctx', 'mp'), may hold values from 0 to 255, as said below
- out_weight: bfloat16 [5120, 3072], P('ctx', 'mp'), may hold values from -0.8984375 to 0.8984375
Outputs:
- projected: bfloat16 [16384, 3072], P('ctx', 'mp')
The draws below stay inside these ranges and needn't reach their ends.
Inputs may be any that keep to these rules, and one draw needn't show every extreme that they name: Each list kept_rows[b, g] holds 128 distinct row numbers of its block, in rising order.
All inputs are finite; a program needn't handle non-finite values.
Results may differ from the reference program's by a relative error of at most 0.011.
Values may be sent and summed in bfloat16 or wider, within the bound.
No kernel may reach another device: no remote copies, remote signals or barrier semaphores. Data moves between devices by JAX's collectives and lax.ppermute only.
A program may use at most 64 MiB of HBM per device.

```python
import jax
import jax.numpy as jnp
from jax import lax

QH = 40
KV = 8
HD = 128
DOUT = 3072
BLOCK = 256
ANCHOR = 128
PASS = 128
TOKENS = 16384
N_CTX = 64


def draw_queries(key, part):
    key = jax.random.fold_in(key, 1)
    base = jnp.clip(jax.random.normal(jax.random.fold_in(key, 2), (TOKENS, QH * HD), jnp.float32), -4.0, 4.0)
    return base.astype(jnp.bfloat16)


def draw_keys(key, part):
    key = jax.random.fold_in(key, 7)
    base = 2.0 * jnp.clip(jax.random.normal(jax.random.fold_in(key, 2), (TOKENS, KV * HD), jnp.float32), -4.0, 4.0)
    return base.astype(jnp.bfloat16)


def draw_kept_rows(key, part):
    key = jax.random.fold_in(key, 5)
    split_keys = jax.random.split(key, N_CTX * KV)
    chosen = jax.vmap(lambda single_key: jax.random.permutation(single_key, BLOCK)[:PASS])(split_keys)
    return jnp.sort(chosen, axis=-1).reshape(N_CTX, KV, PASS).astype(jnp.int32)


def level_of(own_key, extent, cuts, least, top_value):
    factor_of = 1.0
    for axis_at, blocks in cuts:
        heights = jax.random.uniform(jax.random.fold_in(jax.random.fold_in(own_key, 6), axis_at), (blocks,), jnp.float32, least / len(cuts), top_value / len(cuts))
        factor_of = factor_of * jnp.repeat(jnp.exp(heights), extent[axis_at] // blocks).reshape((-1,) + (1,) * (len(extent) - 1 - axis_at))
    return factor_of


def scatter_about(rng, extent, deviation, most, cuts=(), held_as=jnp.bfloat16):
    drawn = jax.random.normal(rng, extent, jnp.float32) * deviation
    if len(cuts) > 0:
        drawn = level_of(rng, extent, cuts, -0.22, 0.18) * drawn
    return jnp.clip(drawn, min=-most, max=most).astype(held_as)


def setup_inputs(seed: int = 0) -> dict:
    key_of = jax.random.split(jax.random.key(seed), 6)
    return {
        "queries": draw_queries(jax.random.fold_in(key_of[5], 71), 0),
        "keys": draw_keys(jax.random.fold_in(key_of[5], 71), 0),
        "values": scatter_about(key_of[2], (TOKENS, KV * HD), 1.0, 6.0, ((0, 64), (1, 8))),
        "kept_rows": draw_kept_rows(jax.random.fold_in(key_of[5], 71), 0),
        "out_weight": scatter_about(key_of[4], (QH * HD, DOUT), 0.15, 0.8984375, ((0, 64), (1, 8))),
    }


masked_score = -1e30


def reference(queries, keys, values, kept_rows, out_weight):
    group = QH // KV
    score_scale = HD ** -0.5
    query_heads = queries.reshape(N_CTX, BLOCK, KV, group, HD)
    key_heads = keys.reshape(N_CTX, BLOCK, KV, HD)
    value_heads = values.reshape(N_CTX, BLOCK, KV, HD)
    anchor_keys = key_heads[0, :ANCHOR]
    anchor_vals = value_heads[0, :ANCHOR]
    picker = jnp.transpose(kept_rows, (0, 2, 1))[..., None].astype(jnp.int32)
    pass_keys = jnp.take_along_axis(key_heads, picker, axis=1).reshape(N_CTX * PASS, KV, HD)
    pass_vals = jnp.take_along_axis(value_heads, picker, axis=1).reshape(N_CTX * PASS, KV, HD)
    source_host = jnp.arange(N_CTX * PASS, dtype=jnp.int32) // PASS
    positions = jnp.arange(BLOCK, dtype=jnp.int32)

    def one_host(host_idx):
        grouped = query_heads[host_idx].astype(jnp.float32)
        all_keys = jnp.concatenate([anchor_keys, key_heads[host_idx], pass_keys], 0).astype(jnp.float32)
        all_vals = jnp.concatenate([anchor_vals, value_heads[host_idx], pass_vals], 0).astype(jnp.float32)
        visible = jnp.concatenate([
            jnp.broadcast_to(host_idx > 0, (BLOCK, ANCHOR)),
            positions[:, None] >= positions[None, :],
            jnp.broadcast_to(source_host[None, :] < host_idx, (BLOCK, N_CTX * PASS))], 1)
        scores = jnp.einsum('rhgd,khd->hgrk', grouped, all_keys) * score_scale
        scores = jnp.where(visible[None, None], scores, masked_score)
        row_max = jnp.max(scores, axis=-1, keepdims=True)
        weights = jnp.exp(scores - row_max)
        denominator = jnp.sum(weights, axis=-1)
        rounded = weights.astype(jnp.bfloat16).astype(jnp.float32)
        summed = jnp.einsum('hgrk,khd->hgrd', rounded, all_vals) / denominator[..., None]
        return jnp.transpose(summed, (2, 0, 1, 3)).reshape(BLOCK, QH * HD).astype(jnp.bfloat16)

    attended = lax.map(one_host, jnp.arange(N_CTX, dtype=jnp.int32)).reshape(TOKENS, QH * HD)
    return jnp.dot(attended, out_weight, preferred_element_type=jnp.float32).astype(jnp.bfloat16)
```

```python
import functools

import jax
import jax.numpy as jnp
from jax import lax
from jax.experimental import pallas as pl
from jax.experimental.pallas import tpu as pltpu
from jax.sharding import Mesh
from jax.sharding import PartitionSpec as P

HD = 128
GROUP = 5
ROWS = 256
UNIT = 128
HALF = 64
MASKED = -1e30
SCALE = HD**-0.5 * 1.4426950408889634
STATE = HD + 16
VMEM = 48 * 1024 * 1024

FULL = ((0, UNIT, 0), (256, UNIT, 1), (512, UNIT, 2), (768, UNIT, 3), (1024, HALF, 4))
FRONT = ((0, UNIT, 0), (256, UNIT, 1))
BACK = ((0, UNIT, 2), (256, UNIT, 3), (512, HALF, 4))


def vmem():
    return pl.BlockSpec(memory_space=pltpu.VMEM)


def smem():
    return pl.BlockSpec(memory_space=pltpu.SMEM)


def params():
    return pltpu.CompilerParams(vmem_limit_bytes=VMEM)


def pick_kernel(core_ref, kept_ref, keys_ref, vals_ref, other_ref, out_ref):
    rows = lax.broadcasted_iota(jnp.int32, (ROWS, UNIT), 0)
    chosen = jnp.where(rows == kept_ref[...], 1.0, 0.0)
    chosen = jnp.transpose(chosen, (1, 0)).astype(jnp.bfloat16)
    dot = functools.partial(jnp.dot, preferred_element_type=jnp.float32)
    out_ref[0:UNIT, :] = dot(chosen, keys_ref[...]).astype(jnp.bfloat16)
    out_ref[UNIT : 2 * UNIT, :] = dot(chosen, vals_ref[...]).astype(jnp.bfloat16)

    @pl.when(core_ref[0] == 0)
    def _():
        out_ref[256 : 256 + HALF, :] = keys_ref[0:HALF, :]
        out_ref[256 + HALF : 384, :] = vals_ref[0:HALF, :]

    @pl.when(core_ref[0] != 0)
    def _():
        out_ref[256:384, :] = other_ref[...]


def pick(core, kept, keys, vals, other):
    return pl.pallas_call(
        pick_kernel,
        out_shape=jax.ShapeDtypeStruct((384, HD), jnp.bfloat16),
        in_specs=[smem(), vmem(), vmem(), vmem(), vmem()],
        out_specs=vmem(),
        compiler_params=params(),
        name="pick",
    )(core, kept, keys, vals, other)


def attend_kernel(*refs, layouts, sides, first, diag):
    refs = list(refs)
    flags = refs.pop(0)
    queries = [refs.pop(0) for _ in sides]
    own = (refs.pop(0), refs.pop(0)) if diag else None
    bundles = [refs.pop(0) for _ in layouts]
    states = None if first else [refs.pop(0) for _ in sides]
    outs = [refs.pop(0) for _ in sides]
    kcat, vcat, vt = refs
    parts = []
    at = 0
    for size in (UNIT, HALF):
        for which, layout in enumerate(layouts):
            for row, count, flag in layout:
                if count != size:
                    continue
                kcat[at : at + count, :] = bundles[which][row : row + count, :]
                vcat[at : at + count, :] = bundles[which][row + count : row + 2 * count, :]
                parts.append((at, count, which, flag))
                at += count
    if at % UNIT:
        kcat[at : at + HALF, :] = jnp.zeros((HALF, HD), jnp.bfloat16)
        vcat[at : at + HALF, :] = jnp.zeros((HALF, HD), jnp.bfloat16)
        parts.append((at, HALF, None, None))
        at += HALF
    shared = at
    if diag:
        kcat[at : at + ROWS, :] = own[0][...]
        vcat[at : at + ROWS, :] = own[1][...]
        at += ROWS
    vt[0:HD, :] = jnp.transpose(vcat[...].astype(jnp.float32), (1, 0)).astype(jnp.bfloat16)
    vt[HD:STATE, :] = jnp.ones((STATE - HD, at), jnp.bfloat16)

    tiles = [(n, side, head) for n, side in enumerate(sides) for head in range(GROUP)]

    def scores(tile):
        n, side, head = tile
        count = at if side == 0 else shared
        query = queries[n][:, head * HD : (head + 1) * HD]
        return lax.dot_general(
            kcat[0:count, :], query, (((1,), (1,)), ((), ())), preferred_element_type=jnp.float32
        )

    def finish(tile, raw):
        n, side, head = tile
        count = at if side == 0 else shared
        pieces = []
        for start, size, which, flag in parts:
            piece = raw[start : start + size, :]
            if which is None:
                pieces.append(jnp.full_like(piece, MASKED))
            else:
                usable = flags[(which * 2 + side) * 5 + flag]
                pieces.append(jnp.where(usable > 0, piece, MASKED))
        if diag and side == 0:
            key_at = lax.broadcasted_iota(jnp.int32, (ROWS, ROWS), 0)
            row_at = lax.broadcasted_iota(jnp.int32, (ROWS, ROWS), 1)
            pieces.append(jnp.where(key_at <= row_at, raw[shared:at, :], MASKED))
        top = functools.reduce(
            jnp.maximum, [jnp.max(piece, axis=0, keepdims=True) for piece in pieces]
        )
        if not first:
            old_top = states[n][head, HD + 8 : HD + 9, :]
            top = jnp.maximum(top, old_top)
        weights = jnp.concatenate(
            [jnp.exp2((piece - top) * SCALE).astype(jnp.bfloat16) for piece in pieces], 0
        )
        total = jnp.dot(vt[:, 0:count], weights, preferred_element_type=jnp.float32)
        if not first:
            total = total + states[n][head] * jnp.exp2((old_top - top) * SCALE)
        outs[n][head, 0 : HD + 8, :] = total[0 : HD + 8, :]
        outs[n][head, HD + 8 : STATE, :] = jnp.broadcast_to(top, (8, ROWS))

    raw = scores(tiles[0])
    for i, tile in enumerate(tiles):
        following = scores(tiles[i + 1]) if i + 1 < len(tiles) else None
        finish(tile, raw)
        raw = following


def attend(flags, queries, bundles, layouts, states=None, own=None, sides=(0, 1), name="attend"):
    first = states is None
    diag = own is not None
    keys = sum(count for layout in layouts for _, count, _ in layout)
    keys = -(-keys // UNIT) * UNIT + (ROWS if diag else 0)
    inputs = [flags, *queries, *(own or ()), *bundles, *(states or ())]
    state = jax.ShapeDtypeStruct((GROUP, STATE, ROWS), jnp.float32)
    tiles = len(sides) * GROUP
    return pl.pallas_call(
        functools.partial(attend_kernel, layouts=layouts, sides=sides, first=first, diag=diag),
        out_shape=[state] * len(sides),
        in_specs=[smem()] + [vmem()] * (len(inputs) - 1),
        out_specs=[vmem()] * len(sides),
        scratch_shapes=[
            pltpu.VMEM((keys, HD), jnp.bfloat16),
            pltpu.VMEM((keys, HD), jnp.bfloat16),
            pltpu.VMEM((STATE, keys), jnp.bfloat16),
        ],
        compiler_params=params(),
        cost_estimate=pl.CostEstimate(
            flops=8 * tiles * ROWS * keys * HD,
            bytes_accessed=4 * 1024 * 1024,
            transcendentals=tiles * ROWS * keys,
        ),
        name=name,
    )(*inputs)


def merge_kernel(mine_ref, theirs_ref, out_ref):
    for head in range(GROUP):
        top_a = mine_ref[head, HD + 8 : HD + 9, :]
        top_b = theirs_ref[head, HD + 8 : HD + 9, :]
        top = jnp.maximum(top_a, top_b)
        a = jnp.exp2((top_a - top) * SCALE)
        b = jnp.exp2((top_b - top) * SCALE)
        total = mine_ref[head, HD : HD + 1, :] * a + theirs_ref[head, HD : HD + 1, :] * b
        summed = mine_ref[head, 0:HD, :] * a + theirs_ref[head, 0:HD, :] * b
        attended = jnp.transpose(summed / total, (1, 0))
        out_ref[:, head * HD : (head + 1) * HD] = attended.astype(jnp.bfloat16)


def merge(mine, theirs):
    return pl.pallas_call(
        merge_kernel,
        out_shape=jax.ShapeDtypeStruct((ROWS, GROUP * HD), jnp.bfloat16),
        in_specs=[vmem(), vmem()],
        out_specs=vmem(),
        compiler_params=params(),
        name="merge",
    )(mine, theirs)


def project_kernel(at_ref, a0, a1, a2, a3, near_ref, far_ref, near_out, far_out, far_sum):
    step = pl.program_id(0)
    for i, a_ref in enumerate((a0, a1, a2, a3)):

        @pl.when(step == i)
        def _(i=i, a_ref=a_ref):
            near = jnp.dot(a_ref[...], near_ref[0, 0], preferred_element_type=jnp.float32)
            far = jnp.dot(a_ref[...], far_ref[0, 0], preferred_element_type=jnp.float32)
            if i == 0:
                near_out[...] = near
                far_sum[...] = far
            else:
                near_out[...] += near
                far_sum[...] += far
            if i == 3:
                far_out[...] = far_sum[...].astype(jnp.bfloat16)


def project(places, heads, weight):
    depth, width = weight.shape[2:]
    whole = pl.BlockSpec((ROWS, depth), lambda k, at: (0, 0))
    result = pl.BlockSpec((ROWS, width), lambda k, at: (0, 0))
    return pl.pallas_call(
        project_kernel,
        out_shape=[
            jax.ShapeDtypeStruct((ROWS, width), jnp.float32),
            jax.ShapeDtypeStruct((ROWS, width), jnp.bfloat16),
        ],
        grid_spec=pltpu.PrefetchScalarGridSpec(
            num_scalar_prefetch=1,
            grid=(4,),
            in_specs=[
                whole,
                whole,
                whole,
                whole,
                pl.BlockSpec((1, 1, depth, width), lambda k, at: (at[k], at[4], 0, 0)),
                pl.BlockSpec((1, 1, depth, width), lambda k, at: (3 - at[k], 1 - at[4], 0, 0)),
            ],
            out_specs=[result, result],
            scratch_shapes=[pltpu.VMEM((ROWS, width), jnp.float32)],
        ),
        compiler_params=params(),
        name="project",
    )(places, *heads, weight, weight)


def ring(size, distance):
    return [(i, (i + distance) % size) for i in range(size)]


def local(queries, keys, values, kept_rows, out_weight):
    y, z, c, x, h = (lax.axis_index(name) for name in ("y", "z", "c", "x", "h"))
    block = (y * 8 + z) * 2 + c
    swap = ring(2, 1)

    anchor = jnp.concatenate([keys[HALF : 2 * HALF], values[HALF : 2 * HALF]], 0)
    anchor = lax.ppermute(anchor, ("y", "z", "c"), [(0, 1)])
    unit = pick(c.reshape(1), kept_rows.reshape(1, UNIT), keys, values, anchor)

    came = [
        lax.ppermute(unit, "y", [(i, i + d) for i in range(4 - d)]) for d in (1, 2, 3)
    ]
    other_queries = lax.ppermute(queries, "c", swap)

    pairs = []
    for yy in range(4):
        for zz in range(8):
            hh = 0 if zz >= 4 else 1
            pairs.append(((yy * 8 + zz) * 2 + hh, ((3 - yy) * 8 + (zz ^ 4)) * 2 + 1 - hh))
    crossed = lax.ppermute(out_weight, ("y", "z", "h"), pairs)
    stays = (z >= 4) == (h == 1)
    weight = lax.all_gather(
        jnp.where(stays, out_weight, crossed), ("y", "z", "c"), axis=0, tiled=True
    ).reshape(4, 2, 640, out_weight.shape[1])

    first = functools.reduce(
        lambda held, d: jnp.where(y == d, came[d - 1][256:384], held), (1, 2, 3), unit[256:384]
    )
    bundle = jnp.concatenate([unit[:256]] + [part[:256] for part in came] + [first], 0)

    def flags_of(source):
        one = jnp.stack([source < z, y >= 1, y >= 2, y >= 3, source == 0])
        return jnp.concatenate([one, one])

    here = jnp.stack(
        [
            y < 0, y >= 1, y >= 2, y >= 3, (z == 0) & (block != 0),
            c == 0, y >= 1, y >= 2, y >= 3, (z == 0) & (block + 1 - 2 * c != 0),
        ]
    ).astype(jnp.int32)

    def flags_at(step):
        return jnp.concatenate(
            [flags_of((z + 8 - step) % 8), flags_of((z + step) % 8)]
        ).astype(jnp.int32)

    both = (queries, other_queries)
    right = lax.ppermute(bundle, "z", ring(8, 1))
    left = lax.ppermute(bundle, "z", ring(8, 7))
    states = attend(here, both, [bundle], (FULL,), own=(keys, values), name="attend0")
    for step in (1, 2):
        next_right = lax.ppermute(right, "z", ring(8, 1))
        next_left = lax.ppermute(left, "z", ring(8, 7))
        states = attend(
            flags_at(step), both, [right, left], (FULL, FULL), states, name=f"attend{step}"
        )
        right, left = next_right, next_left
    front = lax.ppermute(right[:512], "z", ring(8, 1))
    back = lax.ppermute(left[512:], "z", ring(8, 7))
    states = attend(flags_at(3), both, [right, left], (FULL, FULL), states, name="attend3")
    last = ([front, back], (FRONT, BACK))
    (theirs,) = attend(
        flags_at(4), (other_queries,), *last, (states[1],), sides=(1,), name="attend4b"
    )
    theirs = lax.ppermute(theirs, "c", swap)
    (mine,) = attend(flags_at(4), (queries,), *last, (states[0],), sides=(0,), name="attend4a")
    attended = merge(mine, theirs)

    heads = [attended] + [lax.ppermute(attended, "x", ring(4, d)) for d in (1, 3, 2)]
    places = jnp.stack([x, (x + 3) % 4, (x + 1) % 4, (x + 2) % 4, h]).astype(jnp.int32)
    near, far = project(places, heads, weight)
    return (near + lax.ppermute(far, "h", swap)).astype(jnp.bfloat16)


def solution(mesh):
    fine = Mesh(mesh.devices.reshape(4, 8, 2, 4, 2), ("y", "z", "c", "x", "h"))
    ctx, mp = ("y", "z", "c"), ("x", "h")
    placed = (P(ctx, mp), P(ctx, mp), P(ctx, mp), P(ctx, mp, None), P(ctx, mp))
    return jax.shard_map(
        local, mesh=fine, in_specs=placed, out_specs=P(ctx, mp), check_vma=False
    )
```

```python
import functools

import jax
import jax.numpy as jnp
from jax import lax
from jax.experimental import pallas as pl
from jax.experimental.pallas import tpu as pltpu
from jax.sharding import Mesh
from jax.sharding import PartitionSpec as P

HD = 128
GROUP = 5
ROWS = 256
UNIT = 128
HALF = 64
MASKED = -1e30
SCALE = HD**-0.5 * 1.4426950408889634
STATE = HD + 16
WEIGHT_STEP = 1
VMEM = 20 * 1024 * 1024

FULL = ((0, UNIT, 0), (256, UNIT, 1), (512, UNIT, 2), (768, UNIT, 3), (1024, HALF, 4))
FRONT = ((0, UNIT, 0), (256, UNIT, 1))
BACK = ((0, UNIT, 2), (256, UNIT, 3), (512, HALF, 4))


def vmem():
    return pl.BlockSpec(memory_space=pltpu.VMEM)


def smem():
    return pl.BlockSpec(memory_space=pltpu.SMEM)


def params():
    return pltpu.CompilerParams(vmem_limit_bytes=VMEM)


def hbm():
    return pl.BlockSpec(memory_space=pltpu.HBM)


def load(pairs, sems):
    copies = [pltpu.make_async_copy(src, dst, sems.at[i]) for i, (src, dst) in enumerate(pairs)]
    for copy in copies:
        copy.start()
    return copies


def pick_kernel(core_ref, kept_ref, keys_hbm, vals_hbm, far_keys, far_vals, weight_ref, out_ref, *scratch):
    keys_ref, vals_ref, sems = scratch
    copies = load(((keys_hbm, keys_ref), (vals_hbm, vals_ref)), sems)
    rows = lax.broadcasted_iota(jnp.int32, (ROWS, UNIT), 0)
    chosen = jnp.where(rows == kept_ref[...], 1.0, 0.0)
    chosen = jnp.transpose(chosen, (1, 0)).astype(jnp.bfloat16)
    shard = weight_ref.shape[0]
    for i in range(3):
        at = 384 + i * shard
        out_ref[at : at + shard, :] = weight_ref[:, i * HD : (i + 1) * HD]
    for copy in copies:
        copy.wait()
    dot = functools.partial(jnp.dot, preferred_element_type=jnp.float32)
    out_ref[0:UNIT, :] = dot(chosen, keys_ref[...]).astype(jnp.bfloat16)
    out_ref[UNIT : 2 * UNIT, :] = dot(chosen, vals_ref[...]).astype(jnp.bfloat16)

    @pl.when(core_ref[0] == 0)
    def _():
        out_ref[256 : 256 + HALF, :] = keys_ref[0:HALF, :]
        out_ref[256 + HALF : 384, :] = vals_ref[0:HALF, :]

    @pl.when(core_ref[0] != 0)
    def _():
        out_ref[256 : 256 + HALF, :] = far_keys[HALF : 2 * HALF, :]
        out_ref[256 + HALF : 384, :] = far_vals[HALF : 2 * HALF, :]


def pick(core, kept, keys, vals, far_keys, far_vals, weight):
    return pl.pallas_call(
        pick_kernel,
        out_shape=jax.ShapeDtypeStruct((384 + 3 * weight.shape[0], HD), jnp.bfloat16),
        in_specs=[smem(), vmem(), hbm(), hbm(), vmem(), vmem(), vmem()],
        out_specs=vmem(),
        scratch_shapes=[
            pltpu.VMEM((ROWS, HD), jnp.bfloat16),
            pltpu.VMEM((ROWS, HD), jnp.bfloat16),
            pltpu.SemaphoreType.DMA((2,)),
        ],
        compiler_params=params(),
        name="pick",
    )(core, kept, keys, vals, far_keys, far_vals, weight)


def attend_kernel(*refs, layouts, sides, first, diag):
    refs = list(refs)
    flags = refs.pop(0)
    queries = [refs.pop(0) for _ in sides]
    own = (refs.pop(0), refs.pop(0)) if diag else None
    bundles = [refs.pop(0) for _ in layouts]
    states = None if first else [refs.pop(0) for _ in sides]
    outs = [refs.pop(0) for _ in sides]
    kcat, vcat, vt, held, sems = refs
    pairs = [(queries[n], held.at[n]) for n in range(len(sides))]
    copies = load(pairs, sems)
    parts = []
    at = 0
    for size in (UNIT, HALF):
        for which, layout in enumerate(layouts):
            for row, count, flag in layout:
                if count != size:
                    continue
                kcat[at : at + count, :] = bundles[which][row : row + count, :]
                vcat[at : at + count, :] = bundles[which][row + count : row + 2 * count, :]
                parts.append((at, count, which, flag))
                at += count
    if at % UNIT:
        kcat[at : at + HALF, :] = jnp.zeros((HALF, HD), jnp.bfloat16)
        vcat[at : at + HALF, :] = jnp.zeros((HALF, HD), jnp.bfloat16)
        parts.append((at, HALF, None, None))
        at += HALF
    shared = at
    if diag:
        more = load(
            ((own[0], kcat.at[at : at + ROWS, :]), (own[1], vcat.at[at : at + ROWS, :])),
            sems.at[len(sides) :],
        )
        for copy in more:
            copy.wait()
        at += ROWS
    vt[0:HD, :] = jnp.transpose(vcat[...].astype(jnp.float32), (1, 0)).astype(jnp.bfloat16)
    vt[HD:STATE, :] = jnp.ones((STATE - HD, at), jnp.bfloat16)

    tiles = [(n, side, head) for n, side in enumerate(sides) for head in range(GROUP)]
    for copy in copies:
        copy.wait()

    def scores(tile):
        n, side, head = tile
        count = at if side == 0 else shared
        query = held[n, :, head * HD : (head + 1) * HD]
        return lax.dot_general(
            kcat[0:count, :], query, (((1,), (1,)), ((), ())), preferred_element_type=jnp.float32
        )

    def finish(tile, raw):
        n, side, head = tile
        count = at if side == 0 else shared
        pieces = []
        for start, size, which, flag in parts:
            piece = raw[start : start + size, :]
            if which is None:
                pieces.append(jnp.full_like(piece, MASKED))
            else:
                usable = flags[(which * 2 + side) * 5 + flag]
                pieces.append(jnp.where(usable > 0, piece, MASKED))
        if diag and side == 0:
            key_at = lax.broadcasted_iota(jnp.int32, (ROWS, ROWS), 0)
            row_at = lax.broadcasted_iota(jnp.int32, (ROWS, ROWS), 1)
            pieces.append(jnp.where(key_at <= row_at, raw[shared:at, :], MASKED))
        top = functools.reduce(
            jnp.maximum, [jnp.max(piece, axis=0, keepdims=True) for piece in pieces]
        )
        if not first:
            old_top = states[n][head, HD + 8 : HD + 9, :]
            top = jnp.maximum(top, old_top)
        weights = jnp.concatenate(
            [jnp.exp2((piece - top) * SCALE).astype(jnp.bfloat16) for piece in pieces], 0
        )
        total = jnp.dot(vt[:, 0:count], weights, preferred_element_type=jnp.float32)
        if not first:
            total = total + states[n][head] * jnp.exp2((old_top - top) * SCALE)
        outs[n][head, 0 : HD + 8, :] = total[0 : HD + 8, :]
        outs[n][head, HD + 8 : STATE, :] = jnp.broadcast_to(top, (8, ROWS))

    raw = scores(tiles[0])
    for i, tile in enumerate(tiles):
        following = scores(tiles[i + 1]) if i + 1 < len(tiles) else None
        finish(tile, raw)
        raw = following


def attend(flags, queries, bundles, layouts, states=None, own=None, sides=(0, 1), name="attend"):
    first = states is None
    diag = own is not None
    keys = sum(count for layout in layouts for _, count, _ in layout)
    keys = -(-keys // UNIT) * UNIT + (ROWS if diag else 0)
    inputs = [flags, *queries, *(own or ()), *bundles, *(states or ())]
    state = jax.ShapeDtypeStruct((GROUP, STATE, ROWS), jnp.float32)
    tiles = len(sides) * GROUP
    return pl.pallas_call(
        functools.partial(attend_kernel, layouts=layouts, sides=sides, first=first, diag=diag),
        out_shape=[state] * len(sides),
        in_specs=[smem()]
        + [hbm()] * (len(sides) + (2 if diag else 0))
        + [vmem()] * (len(inputs) - 1 - len(sides) - (2 if diag else 0)),
        out_specs=[vmem()] * len(sides),
        scratch_shapes=[
            pltpu.VMEM((keys, HD), jnp.bfloat16),
            pltpu.VMEM((keys, HD), jnp.bfloat16),
            pltpu.VMEM((STATE, keys), jnp.bfloat16),
            pltpu.VMEM((len(sides), ROWS, GROUP * HD), jnp.bfloat16),
            pltpu.SemaphoreType.DMA((len(sides) + 2,)),
        ],
        compiler_params=params(),
        cost_estimate=pl.CostEstimate(
            flops=8 * tiles * ROWS * keys * HD,
            bytes_accessed=4 * 1024 * 1024,
            transcendentals=tiles * ROWS * keys,
        ),
        name=name,
    )(*inputs)


def merge_kernel(mine_ref, theirs_ref, out_ref):
    for head in range(GROUP):
        top_a = mine_ref[head, HD + 8 : HD + 9, :]
        top_b = theirs_ref[head, HD + 8 : HD + 9, :]
        top = jnp.maximum(top_a, top_b)
        a = jnp.exp2((top_a - top) * SCALE)
        b = jnp.exp2((top_b - top) * SCALE)
        total = mine_ref[head, HD : HD + 1, :] * a + theirs_ref[head, HD : HD + 1, :] * b
        summed = mine_ref[head, 0:HD, :] * a + theirs_ref[head, 0:HD, :] * b
        attended = jnp.transpose(summed / total, (1, 0))
        out_ref[:, head * HD : (head + 1) * HD] = attended.astype(jnp.bfloat16)


def merge(mine, theirs):
    return pl.pallas_call(
        merge_kernel,
        out_shape=jax.ShapeDtypeStruct((ROWS, GROUP * HD), jnp.bfloat16),
        in_specs=[vmem(), vmem()],
        out_specs=vmem(),
        compiler_params=params(),
        name="merge",
    )(mine, theirs)


def project_kernel(at_ref, *refs, count, side, first):
    refs = list(refs)
    heads = [refs.pop(0) for _ in range(count)]
    weight = refs.pop(0)
    start = None if first else refs.pop(0)
    out, held, sems = refs
    depth, width = heads[0].shape[1], held.shape[-1]
    half = at_ref[count]
    pairs = []
    for i in range(count):
        at = at_ref[i]
        place = (half, at) if side == "near" else (1 - half, 3 - at)
        for n in range(width // HD):
            source = weight.at[place[0], :, place[1], n]
            pairs.append((source, held.at[i, :, :, n * HD : (n + 1) * HD]))
    copies = load(pairs, sems)
    total = 0.0 if first else start[...]
    for i in range(count):
        for copy in copies[3 * i : 3 * i + 3]:
            copy.wait()
        block = held[i].reshape(depth, width)
        total += jnp.dot(heads[i][...], block, preferred_element_type=jnp.float32)
    out[...] = total.astype(out.dtype)


def project(places, heads, weight, side, start=None, dtype=jnp.float32, name="project"):
    count = len(heads)
    shards, shard, width = weight.shape[1], weight.shape[4], weight.shape[3] * HD
    first = start is None
    return pl.pallas_call(
        functools.partial(project_kernel, count=count, side=side, first=first),
        out_shape=jax.ShapeDtypeStruct((ROWS, width), dtype),
        in_specs=[smem()] + [vmem()] * count + [hbm()] + [vmem()] * (0 if first else 1),
        out_specs=vmem(),
        scratch_shapes=[
            pltpu.VMEM((count, shards, shard, width), jnp.bfloat16),
            pltpu.SemaphoreType.DMA((3 * count,)),
        ],
        compiler_params=params(),
        cost_estimate=pl.CostEstimate(
            flops=2 * ROWS * GROUP * HD * width * count,
            bytes_accessed=2 * GROUP * HD * width * count,
            transcendentals=0,
        ),
        name=name,
    )(places, *heads, weight, *(() if first else (start,)))


def ring(size, distance):
    return [(i, (i + distance) % size) for i in range(size)]


def local(queries, keys, values, kept_rows, out_weight):
    y, z, c, x, h = (lax.axis_index(name) for name in ("y", "z", "c", "x", "h"))
    block = (y * 8 + z) * 2 + c
    swap = ring(2, 1)

    first_block = [(0, 1)]
    anchor = [lax.ppermute(block, ("y", "z", "c"), first_block) for block in (keys, values)]

    pairs = []
    for yy in range(4):
        for zz in range(8):
            hh = 0 if zz >= 4 else 1
            pairs.append(((yy * 8 + zz) * 2 + hh, ((3 - yy) * 8 + (zz ^ 4)) * 2 + 1 - hh))
    crossed = lax.ppermute(out_weight, ("y", "z", "h"), pairs)
    crossed = jnp.where((z >= 4) == (h == 1), out_weight, crossed)
    other_queries = lax.ppermute(queries, "c", swap)

    unit = pick(c.reshape(1), kept_rows.reshape(1, UNIT), keys, values, *anchor, crossed)
    unit, other_queries = lax.optimization_barrier((unit, other_queries))
    line = lax.all_gather(unit, "y", axis=0, tiled=False)
    bundle = jnp.concatenate([line[:, :256].reshape(1024, HD), line[0, 256:384]], 0)
    def flags_of(source):
        one = jnp.stack([(y > i) | ((y == i) & (source < z)) for i in range(4)] + [source == 0])
        return jnp.concatenate([one, one])

    here = jnp.stack(
        [y > i for i in range(4)]
        + [(z == 0) & (block != 0)]
        + [(y > i) | ((y == i) & (c == 0)) for i in range(4)]
        + [(z == 0) & (block + 1 - 2 * c != 0)]
    ).astype(jnp.int32)

    def flags_at(step):
        return jnp.concatenate(
            [flags_of((z + 8 - step) % 8), flags_of((z + step) % 8)]
        ).astype(jnp.int32)

    both = (queries, other_queries)
    right = lax.ppermute(bundle, "z", ring(8, 1))
    left = lax.ppermute(bundle, "z", ring(8, 7))
    states = attend(here, both, [bundle], (FULL,), own=(keys, values), name="attend0")
    rows = line[:, 384:]
    for step in (1, 2):
        if step == WEIGHT_STEP:
            right, left, rows, states = lax.optimization_barrier((right, left, rows, states))
        next_right = lax.ppermute(right, "z", ring(8, 1))
        next_left = lax.ppermute(left, "z", ring(8, 7))
        states = attend(
            flags_at(step), both, [right, left], (FULL, FULL), states, name=f"attend{step}"
        )
        right, left = next_right, next_left
    if WEIGHT_STEP == 3:
        right, rows = lax.optimization_barrier((right, rows))
    weight = lax.all_gather(rows, ("z", "c"), axis=0, tiled=False)
    front = lax.ppermute(right[:512], "z", ring(8, 1))
    back = lax.ppermute(left[512:], "z", ring(8, 7))
    states = attend(flags_at(3), both, [right, left], (FULL, FULL), states, name="attend3")
    last = ([front, back], (FRONT, BACK))
    (theirs,) = attend(
        flags_at(4), (other_queries,), *last, (states[1],), sides=(1,), name="attend4b"
    )
    theirs = lax.ppermute(theirs, "c", swap)
    (mine,) = attend(flags_at(4), (queries,), *last, (states[0],), sides=(0,), name="attend4a")
    attended = merge(mine, theirs)

    weight = weight.reshape(2, 8, 4, 3, out_weight.shape[0], HD)
    nearby = jnp.stack([x, h]).astype(jnp.int32)
    across = jnp.stack([(x + 3) % 4, (x + 1) % 4, (x + 2) % 4, h]).astype(jnp.int32)
    gathered = [lax.ppermute(attended, "x", ring(4, d)) for d in (1, 3, 2)]
    far = project(nearby, [attended], weight, "far", name="far0")
    near = project(nearby, [attended], weight, "near", name="near0")
    far = project(across, gathered, weight, "far", far, jnp.bfloat16, name="far1")
    crossing = lax.ppermute(far, "h", swap)
    near = project(across, gathered, weight, "near", near, name="near1")
    return (near + crossing).astype(jnp.bfloat16)


def solution(mesh):
    fine = Mesh(mesh.devices.reshape(4, 8, 2, 4, 2), ("y", "z", "c", "x", "h"))
    ctx, mp = ("y", "z", "c"), ("x", "h")
    placed = (P(ctx, mp), P(ctx, mp), P(ctx, mp), P(ctx, mp, None), P(ctx, mp))
    return jax.shard_map(
        local, mesh=fine, in_specs=placed, out_specs=P(ctx, mp), check_vma=False
    )
```

```python
import functools

import jax
import jax.numpy as jnp
from jax import lax
from jax.experimental import pallas as pl
from jax.experimental.pallas import tpu as pltpu
from jax.sharding import Mesh
from jax.sharding import PartitionSpec as P

HD = 128
GROUP = 5
ROWS = 256
UNIT = 128
HALF = 64
MASKED = -1e30
SCALE = HD**-0.5 * 1.4426950408889634
STATE = HD + 16
FAR = 40.0
WEIGHT_STEP = 1
VMEM = 20 * 1024 * 1024

FULL = ((0, UNIT, 0), (256, UNIT, 1), (512, UNIT, 2), (768, UNIT, 3), (1024, HALF, 4))
FRONT = ((0, UNIT, 0), (256, UNIT, 1))
BACK = ((0, UNIT, 2), (256, UNIT, 3), (512, HALF, 4))


def vmem():
    return pl.BlockSpec(memory_space=pltpu.VMEM)


def smem():
    return pl.BlockSpec(memory_space=pltpu.SMEM)


def params():
    return pltpu.CompilerParams(vmem_limit_bytes=VMEM)


def hbm():
    return pl.BlockSpec(memory_space=pltpu.HBM)


def load(pairs, sems):
    copies = [pltpu.make_async_copy(src, dst, sems.at[i]) for i, (src, dst) in enumerate(pairs)]
    for copy in copies:
        copy.start()
    return copies


def pick_kernel(core_ref, kept_ref, keys_hbm, vals_hbm, far_keys, far_vals, weight_ref, out_ref, *scratch):
    keys_ref, vals_ref, sems = scratch
    copies = load(((keys_hbm, keys_ref), (vals_hbm, vals_ref)), sems)
    rows = lax.broadcasted_iota(jnp.int32, (ROWS, UNIT), 0)
    chosen = jnp.where(rows == kept_ref[...], 1.0, 0.0)
    chosen = jnp.transpose(chosen, (1, 0)).astype(jnp.bfloat16)
    shard = weight_ref.shape[0]
    for i in range(3):
        at = 384 + i * shard
        out_ref[at : at + shard, :] = weight_ref[:, i * HD : (i + 1) * HD]
    for copy in copies:
        copy.wait()
    dot = functools.partial(jnp.dot, preferred_element_type=jnp.float32)
    out_ref[0:UNIT, :] = dot(chosen, keys_ref[...]).astype(jnp.bfloat16)
    out_ref[UNIT : 2 * UNIT, :] = dot(chosen, vals_ref[...]).astype(jnp.bfloat16)

    @pl.when(core_ref[0] == 0)
    def _():
        out_ref[256 : 256 + HALF, :] = keys_ref[0:HALF, :]
        out_ref[256 + HALF : 384, :] = vals_ref[0:HALF, :]

    @pl.when(core_ref[0] != 0)
    def _():
        out_ref[256 : 256 + HALF, :] = far_keys[HALF : 2 * HALF, :]
        out_ref[256 + HALF : 384, :] = far_vals[HALF : 2 * HALF, :]


def pick(core, kept, keys, vals, far_keys, far_vals, weight):
    return pl.pallas_call(
        pick_kernel,
        out_shape=jax.ShapeDtypeStruct((384 + 3 * weight.shape[0], HD), jnp.bfloat16),
        in_specs=[smem(), vmem(), hbm(), hbm(), vmem(), vmem(), vmem()],
        out_specs=vmem(),
        scratch_shapes=[
            pltpu.VMEM((ROWS, HD), jnp.bfloat16),
            pltpu.VMEM((ROWS, HD), jnp.bfloat16),
            pltpu.SemaphoreType.DMA((2,)),
        ],
        compiler_params=params(),
        name="pick",
    )(core, kept, keys, vals, far_keys, far_vals, weight)


def attend_kernel(*refs, layouts, sides, first, diag):
    refs = list(refs)
    flags = refs.pop(0)
    queries = [refs.pop(0) for _ in sides]
    own = (refs.pop(0), refs.pop(0)) if diag else None
    bundles = [refs.pop(0) for _ in layouts]
    states = None if first else [refs.pop(0) for _ in sides]
    outs = [refs.pop(0) for _ in sides]
    kcat, vcat, vt, held, sems = refs
    pairs = [(queries[n], held.at[n]) for n in range(len(sides))]
    copies = load(pairs, sems)
    parts = []
    at = 0
    for size in (UNIT, HALF):
        for which, layout in enumerate(layouts):
            for row, count, flag in layout:
                if count != size:
                    continue
                kcat[at : at + count, :] = bundles[which][row : row + count, :]
                vcat[at : at + count, :] = bundles[which][row + count : row + 2 * count, :]
                parts.append((at, count, which, flag))
                at += count
    if at % UNIT:
        kcat[at : at + HALF, :] = jnp.zeros((HALF, HD), jnp.bfloat16)
        vcat[at : at + HALF, :] = jnp.zeros((HALF, HD), jnp.bfloat16)
        parts.append((at, HALF, None, None))
        at += HALF
    shared = at
    if diag:
        more = load(
            ((own[0], kcat.at[at : at + ROWS, :]), (own[1], vcat.at[at : at + ROWS, :])),
            sems.at[len(sides) :],
        )
        for copy in more:
            copy.wait()
        at += ROWS
    vt[0:HD, :] = jnp.transpose(vcat[...].astype(jnp.float32), (1, 0)).astype(jnp.bfloat16)
    vt[HD:STATE, :] = jnp.ones((STATE - HD, at), jnp.bfloat16)

    tiles = [(n, side, head) for n, side in enumerate(sides) for head in range(GROUP)]
    for copy in copies:
        copy.wait()

    def scores(tile):
        n, side, head = tile
        count = at if side == 0 else shared
        query = held[n, :, head * HD : (head + 1) * HD]
        return lax.dot_general(
            kcat[0:count, :], query, (((1,), (1,)), ((), ())), preferred_element_type=jnp.float32
        )

    def finish(tile, raw, exact):
        n, side, head = tile
        count = at if side == 0 else shared
        pieces = []
        for start, size, which, flag in parts:
            piece = raw[start : start + size, :]
            if which is None:
                pieces.append(jnp.full_like(piece, MASKED))
            else:
                usable = flags[(which * 2 + side) * 5 + flag]
                pieces.append(jnp.where(usable > 0, piece, MASKED))
        if diag and side == 0:
            key_at = lax.broadcasted_iota(jnp.int32, (ROWS, ROWS), 0)
            row_at = lax.broadcasted_iota(jnp.int32, (ROWS, ROWS), 1)
            pieces.append(jnp.where(key_at <= row_at, raw[shared:at, :], MASKED))
        if exact:
            top = functools.reduce(
                jnp.maximum, [jnp.max(piece, axis=0, keepdims=True) for piece in pieces]
            )
            if not first:
                old_top = states[n][head, HD + 8 : HD + 9, :]
                old_top = jnp.where(states[n][head, HD : HD + 1, :] > 0.0, old_top, MASKED)
                top = jnp.maximum(top, old_top)
            elif side == 1:
                some = jnp.max(raw[0:8, :], axis=0, keepdims=True)
                top = jnp.where(top > 0.5 * MASKED, top, some)
        else:
            top = states[n][head, HD + 8 : HD + 9, :]
        above = [piece - top for piece in pieces]
        weights = jnp.concatenate(
            [jnp.exp2(piece * SCALE).astype(jnp.bfloat16) for piece in above], 0
        )
        total = jnp.dot(vt[:, 0:count], weights, preferred_element_type=jnp.float32)
        if not first:
            held_sum = states[n][head]
            total = total + (held_sum * jnp.exp2((old_top - top) * SCALE) if exact else held_sum)
        outs[n][head, 0 : HD + 8, :] = total[0 : HD + 8, :]
        outs[n][head, HD + 8 : STATE, :] = jnp.broadcast_to(top, (8, ROWS))
        if exact:
            return None
        folded = [jnp.max(piece.reshape(-1, 8, ROWS), axis=0) for piece in above]
        most = jnp.max(functools.reduce(jnp.maximum, folded), axis=0, keepdims=True)
        if side == 0:
            return most
        low = (held_sum[HD : HD + 1, :] == 0.0) & (most * SCALE < -FAR) & (most > 0.5 * MASKED)
        return jnp.where(low, -MASKED, most)

    def work(exact):
        highest = None
        raw = scores(tiles[0])
        for i, tile in enumerate(tiles):
            following = scores(tiles[i + 1]) if i + 1 < len(tiles) else None
            above = finish(tile, raw, exact)
            if not exact:
                highest = above if highest is None else jnp.maximum(highest, above)
            raw = following
        return highest

    if first:
        work(True)
    else:
        highest = jnp.max(work(False))

        @pl.when(highest * SCALE > FAR)
        def _():
            work(True)


def attend(flags, queries, bundles, layouts, states=None, own=None, sides=(0, 1), name="attend"):
    first = states is None
    diag = own is not None
    keys = sum(count for layout in layouts for _, count, _ in layout)
    keys = -(-keys // UNIT) * UNIT + (ROWS if diag else 0)
    inputs = [flags, *queries, *(own or ()), *bundles, *(states or ())]
    state = jax.ShapeDtypeStruct((GROUP, STATE, ROWS), jnp.float32)
    tiles = len(sides) * GROUP
    return pl.pallas_call(
        functools.partial(attend_kernel, layouts=layouts, sides=sides, first=first, diag=diag),
        out_shape=[state] * len(sides),
        in_specs=[smem()]
        + [hbm()] * (len(sides) + (2 if diag else 0))
        + [vmem()] * (len(inputs) - 1 - len(sides) - (2 if diag else 0)),
        out_specs=[vmem()] * len(sides),
        scratch_shapes=[
            pltpu.VMEM((keys, HD), jnp.bfloat16),
            pltpu.VMEM((keys, HD), jnp.bfloat16),
            pltpu.VMEM((STATE, keys), jnp.bfloat16),
            pltpu.VMEM((len(sides), ROWS, GROUP * HD), jnp.bfloat16),
            pltpu.SemaphoreType.DMA((len(sides) + 2,)),
        ],
        compiler_params=params(),
        cost_estimate=pl.CostEstimate(
            flops=8 * tiles * ROWS * keys * HD,
            bytes_accessed=4 * 1024 * 1024,
            transcendentals=tiles * ROWS * keys,
        ),
        name=name,
    )(*inputs)


def merge_kernel(mine_ref, theirs_ref, out_ref):
    for head in range(GROUP):
        sum_a, sum_b = mine_ref[head, HD : HD + 1, :], theirs_ref[head, HD : HD + 1, :]
        top_a = jnp.where(sum_a > 0.0, mine_ref[head, HD + 8 : HD + 9, :], MASKED)
        top_b = jnp.where(sum_b > 0.0, theirs_ref[head, HD + 8 : HD + 9, :], MASKED)
        top = jnp.maximum(top_a, top_b)
        a = jnp.exp2((top_a - top) * SCALE)
        b = jnp.exp2((top_b - top) * SCALE)
        total = sum_a * a + sum_b * b
        summed = mine_ref[head, 0:HD, :] * a + theirs_ref[head, 0:HD, :] * b
        attended = jnp.transpose(summed / total, (1, 0))
        out_ref[:, head * HD : (head + 1) * HD] = attended.astype(jnp.bfloat16)


def merge(mine, theirs):
    return pl.pallas_call(
        merge_kernel,
        out_shape=jax.ShapeDtypeStruct((ROWS, GROUP * HD), jnp.bfloat16),
        in_specs=[vmem(), vmem()],
        out_specs=vmem(),
        compiler_params=params(),
        name="merge",
    )(mine, theirs)


def project_kernel(at_ref, *refs, count, side, first):
    refs = list(refs)
    heads = [refs.pop(0) for _ in range(count)]
    weight = refs.pop(0)
    start = None if first else refs.pop(0)
    out, held, sems = refs
    depth, width = heads[0].shape[1], held.shape[-1]
    half = at_ref[count]
    pairs = []
    for i in range(count):
        at = at_ref[i]
        place = (half, at) if side == "near" else (1 - half, 3 - at)
        for n in range(width // HD):
            source = weight.at[place[0], :, place[1], n]
            pairs.append((source, held.at[i, :, :, n * HD : (n + 1) * HD]))
    copies = load(pairs, sems)
    total = 0.0 if first else start[...]
    for i in range(count):
        for copy in copies[3 * i : 3 * i + 3]:
            copy.wait()
        block = held[i].reshape(depth, width)
        total += jnp.dot(heads[i][...], block, preferred_element_type=jnp.float32)
    out[...] = total.astype(out.dtype)


def project(places, heads, weight, side, start=None, dtype=jnp.float32, name="project"):
    count = len(heads)
    shards, shard, width = weight.shape[1], weight.shape[4], weight.shape[3] * HD
    first = start is None
    return pl.pallas_call(
        functools.partial(project_kernel, count=count, side=side, first=first),
        out_shape=jax.ShapeDtypeStruct((ROWS, width), dtype),
        in_specs=[smem()] + [vmem()] * count + [hbm()] + [vmem()] * (0 if first else 1),
        out_specs=vmem(),
        scratch_shapes=[
            pltpu.VMEM((count, shards, shard, width), jnp.bfloat16),
            pltpu.SemaphoreType.DMA((3 * count,)),
        ],
        compiler_params=params(),
        cost_estimate=pl.CostEstimate(
            flops=2 * ROWS * GROUP * HD * width * count,
            bytes_accessed=2 * GROUP * HD * width * count,
            transcendentals=0,
        ),
        name=name,
    )(places, *heads, weight, *(() if first else (start,)))


def ring(size, distance):
    return [(i, (i + distance) % size) for i in range(size)]


def local(queries, keys, values, kept_rows, out_weight):
    y, z, c, x, h = (lax.axis_index(name) for name in ("y", "z", "c", "x", "h"))
    block = (y * 8 + z) * 2 + c
    swap = ring(2, 1)

    first_block = [(0, 1)]
    anchor = [lax.ppermute(block, ("y", "z", "c"), first_block) for block in (keys, values)]

    pairs = []
    for yy in range(4):
        for zz in range(8):
            hh = 0 if zz >= 4 else 1
            pairs.append(((yy * 8 + zz) * 2 + hh, ((3 - yy) * 8 + (zz ^ 4)) * 2 + 1 - hh))
    crossed = lax.ppermute(out_weight, ("y", "z", "h"), pairs)
    crossed = jnp.where((z >= 4) == (h == 1), out_weight, crossed)
    other_queries = lax.ppermute(queries, "c", swap)

    unit = pick(c.reshape(1), kept_rows.reshape(1, UNIT), keys, values, *anchor, crossed)
    unit, other_queries = lax.optimization_barrier((unit, other_queries))
    line = lax.all_gather(unit, "y", axis=0, tiled=False)
    bundle = jnp.concatenate([line[:, :256].reshape(1024, HD), line[0, 256:384]], 0)
    def flags_of(source):
        one = jnp.stack([(y > i) | ((y == i) & (source < z)) for i in range(4)] + [source == 0])
        return jnp.concatenate([one, one])

    here = jnp.stack(
        [y > i for i in range(4)]
        + [(z == 0) & (block != 0)]
        + [(y > i) | ((y == i) & (c == 0)) for i in range(4)]
        + [(z == 0) & (block + 1 - 2 * c != 0)]
    ).astype(jnp.int32)

    def flags_at(step):
        return jnp.concatenate(
            [flags_of((z + 8 - step) % 8), flags_of((z + step) % 8)]
        ).astype(jnp.int32)

    both = (queries, other_queries)
    right = lax.ppermute(bundle, "z", ring(8, 1))
    left = lax.ppermute(bundle, "z", ring(8, 7))
    states = attend(here, both, [bundle], (FULL,), own=(keys, values), name="attend0")
    rows = line[:, 384:]
    for step in (1, 2):
        if step == WEIGHT_STEP:
            right, left, rows, states = lax.optimization_barrier((right, left, rows, states))
        next_right = lax.ppermute(right, "z", ring(8, 1))
        next_left = lax.ppermute(left, "z", ring(8, 7))
        states = attend(
            flags_at(step), both, [right, left], (FULL, FULL), states, name=f"attend{step}"
        )
        right, left = next_right, next_left
    if WEIGHT_STEP == 3:
        right, rows = lax.optimization_barrier((right, rows))
    weight = lax.all_gather(rows, ("z", "c"), axis=0, tiled=False)
    front = lax.ppermute(right[:512], "z", ring(8, 1))
    back = lax.ppermute(left[512:], "z", ring(8, 7))
    states = attend(flags_at(3), both, [right, left], (FULL, FULL), states, name="attend3")
    last = ([front, back], (FRONT, BACK))
    (theirs,) = attend(
        flags_at(4), (other_queries,), *last, (states[1],), sides=(1,), name="attend4b"
    )
    theirs = lax.ppermute(theirs, "c", swap)
    (mine,) = attend(flags_at(4), (queries,), *last, (states[0],), sides=(0,), name="attend4a")
    attended = merge(mine, theirs)

    weight = weight.reshape(2, 8, 4, 3, out_weight.shape[0], HD)
    nearby = jnp.stack([x, h]).astype(jnp.int32)
    across = jnp.stack([(x + 3) % 4, (x + 1) % 4, (x + 2) % 4, h]).astype(jnp.int32)
    gathered = [lax.ppermute(attended, "x", ring(4, d)) for d in (1, 3, 2)]
    far = project(nearby, [attended], weight, "far", name="far0")
    near = project(nearby, [attended], weight, "near", name="near0")
    far = project(across, gathered, weight, "far", far, jnp.bfloat16, name="far1")
    crossing = lax.ppermute(far, "h", swap)
    near = project(across, gathered, weight, "near", near, name="near1")
    return (near + crossing).astype(jnp.bfloat16)


def solution(mesh):
    fine = Mesh(mesh.devices.reshape(4, 8, 2, 4, 2), ("y", "z", "c", "x", "h"))
    ctx, mp = ("y", "z", "c"), ("x", "h")
    placed = (P(ctx, mp), P(ctx, mp), P(ctx, mp), P(ctx, mp, None), P(ctx, mp))
    return jax.shard_map(
        local, mesh=fine, in_specs=placed, out_specs=P(ctx, mp), check_vma=False
    )
```

```python
import functools

import jax
import jax.numpy as jnp
from jax import lax
from jax.experimental import pallas as pl
from jax.experimental.pallas import tpu as pltpu
from jax.sharding import Mesh
from jax.sharding import PartitionSpec as P

HD = 128
GROUP = 5
ROWS = 256
UNIT = 128
HALF = 64
MASKED = -1e30
SCALE = HD**-0.5 * 1.4426950408889634
STATE = HD + 16
FAR = 40.0
WEIGHT_STEP = 1
VMEM = 20 * 1024 * 1024

FULL = ((0, UNIT, 0), (256, UNIT, 1), (512, UNIT, 2), (768, UNIT, 3), (1024, HALF, 4))
FRONT = ((0, UNIT, 0), (256, UNIT, 1))
BACK = ((0, UNIT, 2), (256, UNIT, 3), (512, HALF, 4))


def vmem():
    return pl.BlockSpec(memory_space=pltpu.VMEM)


def smem():
    return pl.BlockSpec(memory_space=pltpu.SMEM)


def params():
    return pltpu.CompilerParams(vmem_limit_bytes=VMEM)


def hbm():
    return pl.BlockSpec(memory_space=pltpu.HBM)


def load(pairs, sems):
    copies = [pltpu.make_async_copy(src, dst, sems.at[i]) for i, (src, dst) in enumerate(pairs)]
    for copy in copies:
        copy.start()
    return copies


def pick_kernel(core_ref, kept_ref, keys_hbm, vals_hbm, far_keys, far_vals, weight_ref, out_ref, *scratch):
    keys_ref, vals_ref, sems = scratch
    copies = load(((keys_hbm, keys_ref), (vals_hbm, vals_ref)), sems)
    rows = lax.broadcasted_iota(jnp.int32, (ROWS, UNIT), 0)
    chosen = jnp.where(rows == kept_ref[...], 1.0, 0.0)
    chosen = jnp.transpose(chosen, (1, 0)).astype(jnp.bfloat16)
    shard = weight_ref.shape[0]
    for i in range(3):
        at = 384 + i * shard
        out_ref[at : at + shard, :] = weight_ref[:, i * HD : (i + 1) * HD]
    for copy in copies:
        copy.wait()
    dot = functools.partial(jnp.dot, preferred_element_type=jnp.float32)
    out_ref[0:UNIT, :] = dot(chosen, keys_ref[...]).astype(jnp.bfloat16)
    out_ref[UNIT : 2 * UNIT, :] = dot(chosen, vals_ref[...]).astype(jnp.bfloat16)

    @pl.when(core_ref[0] == 0)
    def _():
        out_ref[256 : 256 + HALF, :] = keys_ref[0:HALF, :]
        out_ref[256 + HALF : 384, :] = vals_ref[0:HALF, :]

    @pl.when(core_ref[0] != 0)
    def _():
        out_ref[256 : 256 + HALF, :] = far_keys[HALF : 2 * HALF, :]
        out_ref[256 + HALF : 384, :] = far_vals[HALF : 2 * HALF, :]


def pick(core, kept, keys, vals, far_keys, far_vals, weight):
    return pl.pallas_call(
        pick_kernel,
        out_shape=jax.ShapeDtypeStruct((384 + 3 * weight.shape[0], HD), jnp.bfloat16),
        in_specs=[smem(), vmem(), hbm(), hbm(), vmem(), vmem(), vmem()],
        out_specs=vmem(),
        scratch_shapes=[
            pltpu.VMEM((ROWS, HD), jnp.bfloat16),
            pltpu.VMEM((ROWS, HD), jnp.bfloat16),
            pltpu.SemaphoreType.DMA((2,)),
        ],
        compiler_params=params(),
        name="pick",
    )(core, kept, keys, vals, far_keys, far_vals, weight)


def attend_kernel(*refs, layouts, sides, first, diag):
    refs = list(refs)
    flags = refs.pop(0)
    queries = [refs.pop(0) for _ in sides]
    own = (refs.pop(0), refs.pop(0)) if diag else None
    bundles = [refs.pop(0) for _ in layouts]
    states = None if first else [refs.pop(0) for _ in sides]
    outs = [refs.pop(0) for _ in sides]
    kcat, vcat, vt, held, sems = refs
    pairs = [(queries[n], held.at[n]) for n in range(len(sides))]
    copies = load(pairs, sems)
    parts = []
    at = 0
    for size in (UNIT, HALF):
        for which, layout in enumerate(layouts):
            for row, count, flag in layout:
                if count != size:
                    continue
                kcat[at : at + count, :] = bundles[which][row : row + count, :]
                vcat[at : at + count, :] = bundles[which][row + count : row + 2 * count, :]
                parts.append((at, count, which, flag))
                at += count
    if at % UNIT:
        kcat[at : at + HALF, :] = jnp.zeros((HALF, HD), jnp.bfloat16)
        vcat[at : at + HALF, :] = jnp.zeros((HALF, HD), jnp.bfloat16)
        parts.append((at, HALF, None, None))
        at += HALF
    shared = at
    if diag:
        more = load(
            ((own[0], kcat.at[at : at + ROWS, :]), (own[1], vcat.at[at : at + ROWS, :])),
            sems.at[len(sides) :],
        )
        for copy in more:
            copy.wait()
        at += ROWS
    vt[0:HD, :] = jnp.transpose(vcat[...].astype(jnp.float32), (1, 0)).astype(jnp.bfloat16)
    vt[HD:STATE, :] = jnp.ones((STATE - HD, at), jnp.bfloat16)

    tiles = [(n, side, head) for n, side in enumerate(sides) for head in range(GROUP)]
    for copy in copies:
        copy.wait()

    def scores(tile):
        n, side, head = tile
        count = at if side == 0 else shared
        query = held[n, :, head * HD : (head + 1) * HD]
        return lax.dot_general(
            kcat[0:count, :], query, (((1,), (1,)), ((), ())), preferred_element_type=jnp.float32
        )

    def finish(tile, raw, exact):
        n, side, head = tile
        count = at if side == 0 else shared
        pieces = []
        for start, size, which, flag in parts:
            piece = raw[start : start + size, :]
            if which is None:
                pieces.append(jnp.full_like(piece, MASKED))
            else:
                usable = flags[(which * 2 + side) * 5 + flag]
                pieces.append(jnp.where(usable > 0, piece, MASKED))
        if diag and side == 0:
            key_at = lax.broadcasted_iota(jnp.int32, (ROWS, ROWS), 0)
            row_at = lax.broadcasted_iota(jnp.int32, (ROWS, ROWS), 1)
            pieces.append(jnp.where(key_at <= row_at, raw[shared:at, :], MASKED))
        if exact:
            top = functools.reduce(
                jnp.maximum, [jnp.max(piece, axis=0, keepdims=True) for piece in pieces]
            )
            if not first:
                old_top = states[n][head, HD + 8 : HD + 9, :]
                old_top = jnp.where(states[n][head, HD : HD + 1, :] > 0.0, old_top, MASKED)
                top = jnp.maximum(top, old_top)
            elif side == 1:
                some = jnp.max(raw[0:8, :], axis=0, keepdims=True)
                top = jnp.where(top > 0.5 * MASKED, top, some)
        else:
            top = states[n][head, HD + 8 : HD + 9, :]
        above = [piece - top for piece in pieces]
        weights = jnp.concatenate(
            [jnp.exp2(piece * SCALE).astype(jnp.bfloat16) for piece in above], 0
        )
        total = jnp.dot(vt[:, 0:count], weights, preferred_element_type=jnp.float32)
        if not first:
            held_sum = states[n][head]
            total = total + (held_sum * jnp.exp2((old_top - top) * SCALE) if exact else held_sum)
        outs[n][head, 0 : HD + 8, :] = total[0 : HD + 8, :]
        outs[n][head, HD + 8 : STATE, :] = jnp.broadcast_to(top, (8, ROWS))
        if exact:
            return None
        folded = [jnp.max(piece.reshape(-1, 8, ROWS), axis=0) for piece in above]
        most = jnp.max(functools.reduce(jnp.maximum, folded), axis=0, keepdims=True)
        if side == 0:
            return most
        low = (held_sum[HD : HD + 1, :] == 0.0) & (most * SCALE < -FAR) & (most > 0.5 * MASKED)
        return jnp.where(low, -MASKED, most)

    def work(exact):
        highest = None
        raw = scores(tiles[0])
        for i, tile in enumerate(tiles):
            following = scores(tiles[i + 1]) if i + 1 < len(tiles) else None
            above = finish(tile, raw, exact)
            if not exact:
                highest = above if highest is None else jnp.maximum(highest, above)
            raw = following
        return highest

    if first:
        work(True)
    else:
        highest = jnp.max(work(False))

        @pl.when(highest * SCALE > FAR)
        def _():
            work(True)


def attend(flags, queries, bundles, layouts, states=None, own=None, sides=(0, 1), name="attend"):
    first = states is None
    diag = own is not None
    keys = sum(count for layout in layouts for _, count, _ in layout)
    keys = -(-keys // UNIT) * UNIT + (ROWS if diag else 0)
    inputs = [flags, *queries, *(own or ()), *bundles, *(states or ())]
    state = jax.ShapeDtypeStruct((GROUP, STATE, ROWS), jnp.float32)
    tiles = len(sides) * GROUP
    return pl.pallas_call(
        functools.partial(attend_kernel, layouts=layouts, sides=sides, first=first, diag=diag),
        out_shape=[state] * len(sides),
        in_specs=[smem()]
        + [hbm()] * (len(sides) + (2 if diag else 0))
        + [vmem()] * (len(inputs) - 1 - len(sides) - (2 if diag else 0)),
        out_specs=[vmem()] * len(sides),
        scratch_shapes=[
            pltpu.VMEM((keys, HD), jnp.bfloat16),
            pltpu.VMEM((keys, HD), jnp.bfloat16),
            pltpu.VMEM((STATE, keys), jnp.bfloat16),
            pltpu.VMEM((len(sides), ROWS, GROUP * HD), jnp.bfloat16),
            pltpu.SemaphoreType.DMA((len(sides) + 2,)),
        ],
        compiler_params=params(),
        cost_estimate=pl.CostEstimate(
            flops=8 * tiles * ROWS * keys * HD,
            bytes_accessed=4 * 1024 * 1024,
            transcendentals=tiles * ROWS * keys,
        ),
        name=name,
    )(*inputs)


def merge_kernel(mine_ref, theirs_ref, out_ref):
    for head in range(GROUP):
        sum_a, sum_b = mine_ref[head, HD : HD + 1, :], theirs_ref[head, HD : HD + 1, :]
        top_a = jnp.where(sum_a > 0.0, mine_ref[head, HD + 8 : HD + 9, :], MASKED)
        top_b = jnp.where(sum_b > 0.0, theirs_ref[head, HD + 8 : HD + 9, :], MASKED)
        top = jnp.maximum(top_a, top_b)
        a = jnp.exp2((top_a - top) * SCALE)
        b = jnp.exp2((top_b - top) * SCALE)
        total = sum_a * a + sum_b * b
        summed = mine_ref[head, 0:HD, :] * a + theirs_ref[head, 0:HD, :] * b
        attended = jnp.transpose(summed / total, (1, 0))
        out_ref[:, head * HD : (head + 1) * HD] = attended.astype(jnp.bfloat16)


def merge(mine, theirs):
    return pl.pallas_call(
        merge_kernel,
        out_shape=jax.ShapeDtypeStruct((ROWS, GROUP * HD), jnp.bfloat16),
        in_specs=[vmem(), vmem()],
        out_specs=vmem(),
        compiler_params=params(),
        name="merge",
    )(mine, theirs)


def project_kernel(at_ref, *refs, count, side, first):
    refs = list(refs)
    heads = [refs.pop(0) for _ in range(count)]
    weight = refs.pop(0)
    start = None if first else refs.pop(0)
    out, held, sems = refs
    depth, width = heads[0].shape[1], held.shape[-1]
    half = at_ref[count]
    pairs = []
    for i in range(count):
        at = at_ref[i]
        place = (half, at) if side == "near" else (1 - half, 3 - at)
        for n in range(width // HD):
            source = weight.at[place[0], :, place[1], n]
            pairs.append((source, held.at[i, :, :, n * HD : (n + 1) * HD]))
    copies = load(pairs, sems)
    total = 0.0 if first else start[...]
    for i in range(count):
        for copy in copies[3 * i : 3 * i + 3]:
            copy.wait()
        block = held[i].reshape(depth, width)
        total += jnp.dot(heads[i][...], block, preferred_element_type=jnp.float32)
    out[...] = total.astype(out.dtype)


def project(places, heads, weight, side, start=None, dtype=jnp.float32, name="project"):
    count = len(heads)
    shards, shard, width = weight.shape[1], weight.shape[4], weight.shape[3] * HD
    first = start is None
    return pl.pallas_call(
        functools.partial(project_kernel, count=count, side=side, first=first),
        out_shape=jax.ShapeDtypeStruct((ROWS, width), dtype),
        in_specs=[smem()] + [vmem()] * count + [hbm()] + [vmem()] * (0 if first else 1),
        out_specs=vmem(),
        scratch_shapes=[
            pltpu.VMEM((count, shards, shard, width), jnp.bfloat16),
            pltpu.SemaphoreType.DMA((3 * count,)),
        ],
        compiler_params=params(),
        cost_estimate=pl.CostEstimate(
            flops=2 * ROWS * GROUP * HD * width * count,
            bytes_accessed=2 * GROUP * HD * width * count,
            transcendentals=0,
        ),
        name=name,
    )(places, *heads, weight, *(() if first else (start,)))


def ring(size, distance):
    return [(i, (i + distance) % size) for i in range(size)]


def local(queries, keys, values, kept_rows, out_weight):
    y, z, c, x, h = (lax.axis_index(name) for name in ("y", "z", "c", "x", "h"))
    block = (y * 8 + z) * 2 + c
    swap = ring(2, 1)

    first_block = [(0, 1)]
    anchor = [lax.ppermute(block, ("y", "z", "c"), first_block) for block in (keys, values)]

    pairs = []
    for yy in range(4):
        for zz in range(8):
            hh = 0 if zz >= 4 else 1
            pairs.append(((yy * 8 + zz) * 2 + hh, ((3 - yy) * 8 + (zz ^ 4)) * 2 + 1 - hh))
    crossed = lax.ppermute(out_weight, ("y", "z", "h"), pairs)
    crossed = jnp.where((z >= 4) == (h == 1), out_weight, crossed)
    other_queries = lax.ppermute(queries, "c", swap)

    unit = pick(c.reshape(1), kept_rows.reshape(1, UNIT), keys, values, *anchor, crossed)
    unit, other_queries = lax.optimization_barrier((unit, other_queries))
    line = lax.all_gather(unit, "y", axis=0, tiled=False)
    bundle = jnp.concatenate([line[:, :256].reshape(1024, HD), line[0, 256:384]], 0)
    def flags_of(source):
        one = jnp.stack([(y > i) | ((y == i) & (source < z)) for i in range(4)] + [source == 0])
        return jnp.concatenate([one, one])

    here = jnp.stack(
        [y > i for i in range(4)]
        + [(z == 0) & (block != 0)]
        + [(y > i) | ((y == i) & (c == 0)) for i in range(4)]
        + [(z == 0) & (block + 1 - 2 * c != 0)]
    ).astype(jnp.int32)

    def flags_at(step):
        return jnp.concatenate(
            [flags_of((z + 8 - step) % 8), flags_of((z + step) % 8)]
        ).astype(jnp.int32)

    both = (queries, other_queries)
    right = lax.ppermute(bundle, "z", ring(8, 1))
    left = lax.ppermute(bundle, "z", ring(8, 7))
    states = attend(here, both, [bundle], (FULL,), own=(keys, values), name="attend0")
    rows = line[:, 384:]
    for step in (1, 2):
        if step == WEIGHT_STEP:
            right, left, rows, states = lax.optimization_barrier((right, left, rows, states))
        next_right = lax.ppermute(right, "z", ring(8, 1))
        next_left = lax.ppermute(left, "z", ring(8, 7))
        states = attend(
            flags_at(step), both, [right, left], (FULL, FULL), states, name=f"attend{step}"
        )
        right, left = next_right, next_left
    if WEIGHT_STEP == 3:
        right, rows = lax.optimization_barrier((right, rows))
    weight = lax.all_gather(rows, ("z", "c"), axis=0, tiled=False)
    front = lax.ppermute(right[:512], "z", ring(8, 1))
    back = lax.ppermute(left[512:], "z", ring(8, 7))
    states = attend(flags_at(3), both, [right, left], (FULL, FULL), states, name="attend3")
    last = ([front, back], (FRONT, BACK))
    (theirs,) = attend(
        flags_at(4), (other_queries,), *last, (states[1],), sides=(1,), name="attend4b"
    )
    theirs = lax.ppermute(theirs, "c", swap)
    (mine,) = attend(flags_at(4), (queries,), *last, (states[0],), sides=(0,), name="attend4a")
    attended = merge(mine, theirs)

    weight = weight.reshape(2, 8, 4, 3, out_weight.shape[0], HD)
    nearby = jnp.stack([x, h]).astype(jnp.int32)
    across = jnp.stack([(x + 2) % 4, (x + 3) % 4, (x + 1) % 4, h]).astype(jnp.int32)
    gathered = [lax.ppermute(attended, "x", ring(4, d)) for d in (2, 1, 3)]
    far = project(nearby, [attended], weight, "far", name="far0")
    near = project(nearby, [attended], weight, "near", name="near0")
    far = project(across, gathered, weight, "far", far, jnp.bfloat16, name="far1")
    crossing = lax.ppermute(far, "h", swap)
    near = project(across, gathered, weight, "near", near, name="near1")
    return (near + crossing).astype(jnp.bfloat16)


def solution(mesh):
    fine = Mesh(mesh.devices.reshape(4, 8, 2, 4, 2), ("y", "z", "c", "x", "h"))
    ctx, mp = ("y", "z", "c"), ("x", "h")
    placed = (P(ctx, mp), P(ctx, mp), P(ctx, mp), P(ctx, mp, None), P(ctx, mp))
    return jax.shard_map(
        local, mesh=fine, in_specs=placed, out_specs=P(ctx, mp), check_vma=False
    )
```
